32 devices in a mesh: dp: 8 (over z, x), tensor: 4 (over y, core).
Axes of the slice: x: 2, y: 2, z: 4, core: 2. Of those that a mesh axis runs over, the one named last changes fastest.
Arguments:
- tokens: bfloat16 [8192, 1024], P(('dp', 'tensor')), may hold values from -6 to 6
- cotangent: bfloat16 [8192, 1024], P(('dp', 'tensor')), may hold values from -6 to 6
- document_index: int32 [8, 1024], P('dp'), may hold values from 0 to 3, as said below
- routes: int32 [8192, 8], P('dp'), may hold values from 0 to 31, all different within a row; in each aligned block of 1024 rows (0 to 1023, 1024 to 2047, ...) at most 512 rows name the same one
- gain_attn: bfloat16 [1024], P(('dp', 'tensor')), may hold values from 0.5 to 1.5
- gain_moe: bfloat16 [1024], P(('dp', 'tensor')), may hold values from 0.5 to 1.5
- w_query: bfloat16 [1024, 1024], P('dp', 'tensor'), may hold values from -0.1875 to 0.1875
- key_weight: bfloat16 [1024, 512], P('dp', 'tensor'), may hold values from -0.1875 to 0.1875
- value_weight: bfloat16 [1024, 512], P('dp', 'tensor'), may hold values from -0.1875 to 0.1875
- w_out: bfloat16 [1024, 1024], P('dp', 'tensor'), may hold values from -0.75 to 0.75
- w_router: bfloat16 [1024, 32], P(('dp', 'tensor')), may hold values from -0.08984375 to 0.08984375
- w_gate: bfloat16 [1024, 32, 512], P('dp', None, 'tensor'), may hold values from -0.1875 to 0.1875
- w_up: bfloat16 [1024, 32, 512], P('dp', None, 'tensor'), may hold values from -0.1875 to 0.1875
- w_down: bfloat16 [1024, 32, 512], P('dp', None, 'tensor'), may hold values from -1 to 1
Outputs:
- output: bfloat16 [8192, 1024], P(('dp', 'tensor'))
- grad_tokens: bfloat16 [8192, 1024], P(('dp', 'tensor'))
- grad_gain_attn: float32 [1024], P(('dp', 'tensor'))
- grad_gain_moe: float32 [1024], P(('dp', 'tensor'))
- grad_query: float32 [1024, 1024], P('dp', 'tensor')
- grad_key: float32 [1024, 512], P('dp', 'tensor')
- grad_value: float32 [1024, 512], P('dp', 'tensor')
- grad_out: float32 [1024, 1024], P('dp', 'tensor')
- grad_router: float32 [1024, 32], P(('dp', 'tensor'))
- grad_gate: float32 [1024, 32, 512], P('dp', None, 'tensor')
- grad_up: float32 [1024, 32, 512], P('dp', None, 'tensor')
- grad_down: float32 [1024, 32, 512], P('dp', None, 'tensor')
The draws below stay inside these ranges and needn't reach their ends.
Inputs may be any that keep to these rules, and one draw needn't show every extreme that they name: `document_index`: along each sequence the numbers start at 0 and never fall; a sequence holds exactly 4 documents of 200 tokens or more each, and the last token has number 4 - 1. `routes`: each row names 8 different experts. In each aligned block of 1024 rows (the tokens of one index of dp) no expert is named by more than 512 rows, a bound that some block reaches.
All inputs are finite; a program needn't handle non-finite values.
Results may differ from the reference program's by a relative error of at most 0.023.
Values may be sent and summed in bfloat16 or wider, within the bound.
A program may use at most 320 MiB of HBM per device.

```python
import math
from functools import partial
import jax
import jax.numpy as jnp
import numpy as np
from jax import lax

MODEL_WIDTH = 1024
QUERY_HEADS = 16
KEY_VALUE_HEADS = 8
HEAD_SIZE = 64
E = 32
TOP = 8
FF = 512
SEQUENCE_LENGTH = 1024
DOCS = 4
MIN_DOC = 200
SEQ_DP = 1
SEQUENCE_COUNT = 8
TOKENS = 8192
CAP = 512


def draw_document_index(key, part):
    key = jax.random.fold_in(key, 11)
    spare = SEQUENCE_LENGTH - DOCS * MIN_DOC
    picks = jax.random.randint(key, (SEQUENCE_COUNT, DOCS - 1), 0, spare + 1)
    picks = jnp.sort(picks, axis=1)
    cuts = picks + MIN_DOC * jnp.arange(1, DOCS, dtype=jnp.int32)[None, :]
    places = jnp.arange(SEQUENCE_LENGTH, dtype=jnp.int32)
    return jnp.sum((cuts[:, :, None] <= places[None, None, :]).astype(jnp.int32), axis=1)


def block_levels(rng, shape, pieces, least, largest):
    level = 1.0
    for axis_at, shards_of in pieces:
        draws = jax.random.uniform(jax.random.fold_in(jax.random.fold_in(rng, 6), axis_at), (shards_of,), jnp.float32, least / len(pieces), largest / len(pieces))
        level = level * jnp.repeat(jnp.exp(draws), shape[axis_at] // shards_of).reshape((-1,) + (1,) * (len(shape) - 1 - axis_at))
    return level


def shared_out(key, own, number, rows, number_of, top, reach, skew):
    order = jax.random.permutation(key, number_of)
    crowded, ordinary = shares(number_of, rows * top, reach, skew, True), shares(number_of, rows * top, reach, skew, False)
    places = jnp.arange(number_of)

    def named(lengths, offset_by):
        used = int((lengths > 0).sum())
        fixed = max(1, used // 4)
        shifted = fixed + (places - fixed + offset_by * (used - fixed)) % max(1, number_of - fixed)
        return jnp.zeros((number_of,), jnp.int32).at[order[jnp.where(places < fixed, places, shifted)]].set(jnp.asarray(lengths, jnp.int32))

    lengths = jnp.where(number % 4 == 0, named(crowded, number // 4), named(ordinary, number - number // 4 - 1))
    mixed = jax.random.permutation(jax.random.fold_in(own, 3), number_of)
    giver, taker = mixed[0:number_of // 2 * 2:2], mixed[1:number_of // 2 * 2:2]
    margin = jnp.minimum(lengths[giver] - 1, reach - lengths[taker]) // 2
    margin = jnp.where((giver == order[0]) | (taker == order[0]) | (lengths[taker] == 0), 0, jnp.maximum(margin, 0))
    shifted = jax.random.randint(jax.random.fold_in(own, 4), (number_of // 2,), 0, 1 << 20) % (margin + 1)
    lengths = lengths.at[giver].add(-shifted).at[taker].add(shifted)
    labels = jnp.searchsorted(jnp.cumsum(lengths), jnp.arange(rows * top), side="right").astype(jnp.int32)
    grid = labels.reshape(top, rows).T
    grid = grid[jax.random.permutation(jax.random.fold_in(own, 1), rows)]
    offset_by = jax.random.randint(jax.random.fold_in(own, 2), (rows, 1), 0, top)
    return jnp.take_along_axis(grid, (jnp.arange(top)[None, :] + offset_by) % top, axis=1)


def shares(count, total, limit, lean, full):
    loads = [(1 << 20) // math.isqrt(standing ** lean) + 1 for standing in range(1, count + 1)]
    largest = limit if full else min(limit, max(-(-total // count), total * loads[0] // sum(loads)))
    least = 1 if total - largest >= count - 1 else 0
    holding, spare = [largest] + [least] * (count - 1), total - largest - least * (count - 1)
    while spare > 0:
        candidates = [i for i in range(1, count) if holding[i] < largest] or [i for i in range(1, count) if holding[i] < limit]
        whole, budget = sum([loads[i] for i in candidates]), spare
        for i in candidates:
            extra = min(limit - holding[i], max(1, budget * loads[i] // whole), spare)
            holding[i] = holding[i] + extra
            spare = spare - extra
    return np.array(holding)


def scatter_about(key, shape, deviation, most, split=(), held_as=jnp.bfloat16):
    values = jax.random.normal(key, shape, jnp.float32) * deviation
    if len(split) > 0:
        values = block_levels(key, shape, split, -0.22, 0.18) * values
    return jnp.clip(values, min=-most, max=most).astype(held_as)


def setup_inputs(seed: int = 0) -> dict:
    arg_keys = jax.random.split(jax.random.key(seed), 15)
    tokens = scatter_about(arg_keys[0], (TOKENS, MODEL_WIDTH), 1.0, 6.0, ((0, 32),))
    cotangent = scatter_about(arg_keys[1], (TOKENS, MODEL_WIDTH), 1.0, 6.0, ((0, 32),))
    document_index = draw_document_index(jax.random.fold_in(arg_keys[14], 71), 0)
    routes_keys = jax.random.split(jax.random.fold_in(arg_keys[3], 1), TOKENS // (SEQ_DP * SEQUENCE_LENGTH))
    routes_turns = jax.random.permutation(jax.random.fold_in(arg_keys[3], 3), TOKENS // (SEQ_DP * SEQUENCE_LENGTH))
    routes = jax.vmap(lambda own, number: shared_out(jax.random.fold_in(arg_keys[3], 2), own, number, SEQ_DP * SEQUENCE_LENGTH, E, TOP, CAP, 1))(routes_keys, routes_turns).reshape((TOKENS, TOP))
    gain_attn = jnp.clip(1.0 + 0.1 * jax.random.normal(arg_keys[4], (MODEL_WIDTH,), jnp.float32), 0.5, 1.5).astype(jnp.bfloat16)
    gain_moe = jnp.clip(1.0 + 0.1 * jax.random.normal(arg_keys[5], (MODEL_WIDTH,), jnp.float32), 0.5, 1.5).astype(jnp.bfloat16)
    w_query = scatter_about(arg_keys[6], (MODEL_WIDTH, QUERY_HEADS * HEAD_SIZE), MODEL_WIDTH ** -0.5, 0.1875, ((0, 8), (1, 4)))
    key_weight = scatter_about(arg_keys[7], (MODEL_WIDTH, KEY_VALUE_HEADS * HEAD_SIZE), MODEL_WIDTH ** -0.5, 0.1875, ((0, 8), (1, 4)))
    value_weight = scatter_about(arg_keys[8], (MODEL_WIDTH, KEY_VALUE_HEADS * HEAD_SIZE), MODEL_WIDTH ** -0.5, 0.1875, ((0, 8), (1, 4)))
    w_out = scatter_about(arg_keys[9], (MODEL_WIDTH, QUERY_HEADS * HEAD_SIZE), (QUERY_HEADS * HEAD_SIZE // 16) ** -0.5, 0.75, ((0, 8), (1, 4)))
    w_router = scatter_about(arg_keys[10], (MODEL_WIDTH, E), 0.015625, 0.08984375, ((0, 32),))
    w_gate = scatter_about(arg_keys[11], (MODEL_WIDTH, E, FF), MODEL_WIDTH ** -0.5, 0.1875, ((0, 8), (2, 4)))
    w_up = scatter_about(arg_keys[12], (MODEL_WIDTH, E, FF), MODEL_WIDTH ** -0.5, 0.1875, ((0, 8), (2, 4)))
    w_down = scatter_about(arg_keys[13], (MODEL_WIDTH, E, FF), (FF // 16) ** -0.5, 1.0, ((0, 8), (2, 4)))
    return {"tokens": tokens, "cotangent": cotangent, "document_index": document_index, "routes": routes, "gain_attn": gain_attn, "gain_moe": gain_moe, "w_query": w_query, "key_weight": key_weight, "value_weight": value_weight, "w_out": w_out, "w_router": w_router, "w_gate": w_gate, "w_up": w_up, "w_down": w_down}


eps_norm = 1e-06
rope_base = 10000.0
highest = lax.Precision.HIGHEST

@jax.custom_vjp
def low(v):
    return lax.optimization_barrier(v.astype(jnp.bfloat16)).astype(jnp.float32)

@jax.custom_vjp
def low_back(v):
    return v

def low_keep(v):
    return (low(v), None)

def low_pass(kept, grad):
    return (grad,)

def back_keep(v):
    return (v, None)

def back_low(kept, grad):
    return (low(grad),)
low.defvjp(low_keep, low_pass)
low_back.defvjp(back_keep, back_low)

def matmul(left, right):
    return jnp.dot(left, right, precision=highest, preferred_element_type=jnp.float32)

def matmul_right_t(left, right):
    return lax.dot_general(left, right, (((1,), (1,)), ((), ())), precision=highest, preferred_element_type=jnp.float32)

def rms_scale(field, gain):
    inverse = lax.rsqrt(lax.optimization_barrier(jnp.mean(field * field, axis=-1, keepdims=True)) + eps_norm)
    return field * inverse * gain

def doc_positions(segment_row):
    places = jnp.arange(segment_row.shape[0], dtype=jnp.int32)
    before = lax.optimization_barrier(jnp.sum((segment_row[None, :] < segment_row[:, None]).astype(jnp.int32), axis=1))
    return places - before

def rotate_pairs(field, token_positions, heads, sign):
    length_tokens = field.shape[0]
    half = HEAD_SIZE // 2
    freqs = rope_base ** (-2.0 * jnp.arange(half, dtype=jnp.float32) / HEAD_SIZE)
    angles = token_positions.astype(jnp.float32)[:, None] * freqs[None, :]
    cosine = jnp.cos(angles)[:, None, :]
    sine = sign * jnp.sin(angles)[:, None, :]
    shaped = field.reshape(length_tokens, heads, HEAD_SIZE)
    first = shaped[:, :, :half]
    second = shaped[:, :, half:]
    turned = jnp.concatenate([first * cosine - second * sine, second * cosine + first * sine], axis=2)
    return turned.reshape(length_tokens, heads * HEAD_SIZE)

def attend_heads(packed):
    query_rows, key, value_rows, segment_row = packed
    length_tokens = query_rows.shape[0]
    query_group = QUERY_HEADS // KEY_VALUE_HEADS
    heads_of_query = query_rows.reshape(length_tokens, KEY_VALUE_HEADS, query_group, HEAD_SIZE)
    heads_of_key = key.reshape(length_tokens, KEY_VALUE_HEADS, HEAD_SIZE)
    heads_of_value = value_rows.reshape(length_tokens, KEY_VALUE_HEADS, HEAD_SIZE)
    raw = jnp.einsum('qkgd,skd->kgqs', heads_of_query, heads_of_key, precision=highest, preferred_element_type=jnp.float32) * HEAD_SIZE ** (-0.5)
    scores = low_back(raw)
    places = jnp.arange(length_tokens, dtype=jnp.int32)
    allowed = (segment_row[None, :] == segment_row[:, None]) & (places[None, :] <= places[:, None])
    scores = jnp.where(allowed[None, None], scores, -1e+30)
    peak = lax.optimization_barrier(jnp.max(scores, axis=-1, keepdims=True))
    weights = jnp.exp(scores - peak)
    probs = low(weights / lax.optimization_barrier(jnp.sum(weights, axis=-1, keepdims=True)))
    mixed = jnp.einsum('kgqs,skd->qkgd', probs, heads_of_value, precision=highest, preferred_element_type=jnp.float32)
    return mixed.reshape(length_tokens, QUERY_HEADS * HEAD_SIZE)

def expert_block(normed, gates, routes, gate_all, up_all, down_all):
    flattened = routes.reshape(-1)
    order = jnp.argsort(flattened, stable=True).astype(jnp.int32)
    member = (flattened[:, None] == jnp.arange(E, dtype=jnp.int32)[None, :]).astype(jnp.int32)
    counts = lax.optimization_barrier(jnp.sum(member, axis=0))
    starts = jnp.cumsum(counts) - counts
    slots = jnp.arange(CAP, dtype=jnp.int32)
    table = order[jnp.minimum(starts[:, None] + slots[None, :], flattened.shape[0] - 1)]
    valid = (slots[None, :] < counts[:, None]).astype(jnp.float32)
    token_of = table // TOP
    route_of = table % TOP

    def one_expert(carry, packed):
        tokens_e, route_e, valid_e, gate_w, up_w, down_w = packed
        inputs = normed[tokens_e]
        gate_pre = low_back(matmul(inputs, gate_w))
        up_pre = low_back(matmul(inputs, up_w))
        active = low(jax.nn.silu(gate_pre) * up_pre)
        result = low_back(matmul_right_t(active, down_w))
        weight = gates[tokens_e, route_e] * valid_e
        return (carry.at[tokens_e].add(weight[:, None] * result), None)
    total, _ = lax.scan(jax.checkpoint(one_expert), jnp.zeros(normed.shape, jnp.float32), (token_of, route_of, valid, gate_all, up_all, down_all))
    return total

def layer(document_index, routes, tokens, gain_attn, gain_moe, w_query, key_weight, value_weight, w_out, w_router, w_gate, w_up, w_down):
    normed = low(rms_scale(tokens, gain_attn))
    query_pre = low_back(matmul(normed, w_query))
    key_before_rotary = low_back(matmul(normed, key_weight))
    value_rows = low(low_back(matmul(normed, value_weight)))
    token_positions = jax.vmap(doc_positions)(document_index).reshape(-1)
    query_rows = low(rotate_pairs(query_pre, token_positions, QUERY_HEADS, 1.0))
    key = low(rotate_pairs(key_before_rotary, token_positions, KEY_VALUE_HEADS, 1.0))
    attended_rows = lax.map(jax.checkpoint(attend_heads), (query_rows.reshape(SEQUENCE_COUNT, SEQUENCE_LENGTH, QUERY_HEADS * HEAD_SIZE), key.reshape(SEQUENCE_COUNT, SEQUENCE_LENGTH, KEY_VALUE_HEADS * HEAD_SIZE), value_rows.reshape(SEQUENCE_COUNT, SEQUENCE_LENGTH, KEY_VALUE_HEADS * HEAD_SIZE), document_index))
    attended_rows = low(low_back(attended_rows.reshape(TOKENS, QUERY_HEADS * HEAD_SIZE)))
    middle = tokens + low_back(matmul_right_t(attended_rows, w_out))
    normed_two = low(rms_scale(middle, gain_moe))
    logits = low_back(matmul(normed_two, w_router))
    picked = jnp.take_along_axis(logits, routes, axis=1)
    gates = low(jax.nn.softmax(picked, axis=-1))
    block_rows = SEQ_DP * SEQUENCE_LENGTH
    blocks = TOKENS // block_rows
    gate_all = jnp.transpose(w_gate, (1, 0, 2))
    up_all = jnp.transpose(w_up, (1, 0, 2))
    down_all = jnp.transpose(w_down, (1, 0, 2))

    def one_block(packed):
        return expert_block(packed[0], packed[1], packed[2], gate_all, up_all, down_all)
    moe = lax.map(jax.checkpoint(one_block), (normed_two.reshape(blocks, block_rows, MODEL_WIDTH), gates.reshape(blocks, block_rows, TOP), routes.reshape(blocks, block_rows, TOP)))
    return middle + low_back(moe.reshape(TOKENS, MODEL_WIDTH))

def reference(tokens, cotangent, document_index, routes, gain_attn, gain_moe, w_query, key_weight, value_weight, w_out, w_router, w_gate, w_up, w_down):
    floats = [array.astype(jnp.float32) for array in (tokens, gain_attn, gain_moe, w_query, key_weight, value_weight, w_out, w_router, w_gate, w_up, w_down)]
    result, pullback = jax.vjp(partial(layer, document_index, routes), *floats)
    gradients = pullback(cotangent.astype(jnp.float32))
    return (result.astype(jnp.bfloat16), gradients[0].astype(jnp.bfloat16), gradients[1], gradients[2], gradients[3], gradients[4], gradients[5], gradients[6], gradients[7], gradients[8], gradients[9], gradients[10])
```

```python
import jax
import jax.numpy as jnp
from jax import lax
from jax.sharding import PartitionSpec as P

HEAD_SIZE = 64


eps_norm = 1e-06
rope_base = 10000.0


def plain_dot(left, right):
    return jnp.dot(left, right, preferred_element_type=jnp.float32)


def dot_right_t(left, right):
    return lax.dot_general(
        left, right, (((1,), (1,)), ((), ())), preferred_element_type=jnp.float32
    )


def dot_left_t(left, right):
    return lax.dot_general(
        left, right, (((0,), (0,)), ((), ())), preferred_element_type=jnp.float32
    )


def doc_positions(segment_row):
    places = jnp.arange(segment_row.shape[0], dtype=jnp.int32)
    before = jnp.sum((segment_row[None, :] < segment_row[:, None]).astype(jnp.int32), axis=1)
    return places - before


def rotate_pairs(field, token_positions, heads, sign):
    length_tokens = field.shape[0]
    half = HEAD_SIZE // 2
    freqs = rope_base ** (-2.0 * jnp.arange(half, dtype=jnp.float32) / HEAD_SIZE)
    angles = token_positions.astype(jnp.float32)[:, None] * freqs[None, :]
    cosine = jnp.cos(angles)[:, None, :]
    sine = sign * jnp.sin(angles)[:, None, :]
    shaped = field.reshape(length_tokens, heads, HEAD_SIZE)
    first = shaped[:, :, :half]
    second = shaped[:, :, half:]
    turned = jnp.concatenate(
        [first * cosine - second * sine, second * cosine + first * sine], axis=2
    )
    return turned.reshape(length_tokens, heads * HEAD_SIZE)


def norm_backward(field, inverse, gain, upstream):
    scaled = upstream * gain
    gain_grad = jnp.sum(upstream * field * inverse, axis=0)
    inner = jnp.mean(scaled * field, axis=1, keepdims=True)
    return (inverse * scaled - field * inverse**3 * inner, gain_grad)


def body(
    tokens,
    cotangent,
    document_index,
    routes,
    gain_attn,
    gain_moe,
    w_query,
    key_weight,
    value_weight,
    w_out,
    w_router,
    w_gate,
    w_up,
    w_down,
):
    parts = lax.axis_size("tensor")
    local_rows = tokens.shape[0]
    group_rows = local_rows * parts
    width = tokens.shape[1]
    sequences = document_index.shape[0]
    length_tokens = document_index.shape[1]
    my_index = lax.axis_index("tensor")
    experts = w_gate.shape[1]
    scale = HEAD_SIZE ** (-0.5)
    ff_local = w_gate.shape[2]
    small_packed = jnp.concatenate([w_router, gain_attn[:, None], gain_moe[:, None]], axis=1)
    small_full = lax.all_gather(small_packed, ("dp", "tensor"), axis=0, tiled=True)
    router_full = small_full[:, :experts]
    gain_one_f = small_full[:, experts].astype(jnp.float32)
    gain_two_f = small_full[:, experts + 1].astype(jnp.float32)
    tokens_all = lax.all_gather(tokens, "tensor", axis=0, tiled=True)
    attn_full = lax.all_gather(
        jnp.concatenate([w_query, key_weight, value_weight, w_out], axis=1),
        "dp",
        axis=0,
        tiled=True,
    )
    q_width = w_query.shape[1]
    kv_width = key_weight.shape[1]
    joined_width = q_width + 2 * kv_width
    joined = attn_full[:, :joined_width]
    full_out = attn_full[:, joined_width:]
    full_gate, full_up, full_down = (
        lax.all_gather(w_gate.reshape(-1, experts * ff_local), "dp", axis=0, tiled=True),
        lax.all_gather(w_up.reshape(-1, experts * ff_local), "dp", axis=0, tiled=True),
        lax.all_gather(w_down.reshape(-1, experts * ff_local), "dp", axis=0, tiled=True),
    )
    moe_grads_all = lax.all_gather(cotangent, "tensor", axis=0, tiled=True)
    tokens_f = tokens.astype(jnp.float32)
    inverse_one = lax.rsqrt(jnp.mean(tokens_f * tokens_f, axis=1, keepdims=True) + eps_norm)
    tokens_all_f = tokens_all.astype(jnp.float32)
    inverse_all = lax.rsqrt(
        jnp.mean(tokens_all_f * tokens_all_f, axis=1, keepdims=True) + eps_norm
    )
    normed_all = (tokens_all_f * inverse_all * gain_one_f).astype(jnp.bfloat16)
    heads_q = q_width // HEAD_SIZE
    heads_kv = kv_width // HEAD_SIZE
    query_group = heads_q // heads_kv
    projected = plain_dot(normed_all, joined)
    token_positions = jax.vmap(doc_positions)(document_index).reshape(-1)
    query_b = rotate_pairs(projected[:, :q_width], token_positions, heads_q, 1.0).astype(
        jnp.bfloat16
    )
    key_b = rotate_pairs(
        projected[:, q_width : q_width + kv_width], token_positions, heads_kv, 1.0
    ).astype(jnp.bfloat16)
    value_b = projected[:, q_width + kv_width :].astype(jnp.bfloat16)

    def scores_of(query_s, key_s, segment_s):
        heads_of_query = query_s.reshape(length_tokens, heads_kv, query_group, HEAD_SIZE)
        heads_of_key = key_s.reshape(length_tokens, heads_kv, HEAD_SIZE)
        raw = (
            jnp.einsum(
                "qkgd,skd->kgqs", heads_of_query, heads_of_key, preferred_element_type=jnp.float32
            )
            * scale
        )
        places = jnp.arange(length_tokens, dtype=jnp.int32)
        allowed = (segment_s[None, :] == segment_s[:, None]) & (places[None, :] <= places[:, None])
        return jnp.where(allowed[None, None], raw, -1e30)

    def forward_one(packed):
        query_s, key_s, value_s, segment_s = packed
        masked = scores_of(query_s, key_s, segment_s)
        peak = jnp.max(masked, axis=-1, keepdims=True)
        weights = jnp.exp(masked - peak)
        total = jnp.sum(weights, axis=-1, keepdims=True)
        probs = (weights / total).astype(jnp.bfloat16)
        heads_of_value = value_s.reshape(length_tokens, heads_kv, HEAD_SIZE)
        mixed = jnp.einsum(
            "kgqs,skd->qkgd", probs, heads_of_value, preferred_element_type=jnp.float32
        )
        return (mixed.reshape(length_tokens, q_width).astype(jnp.bfloat16), peak + jnp.log(total))

    query_seq = query_b.reshape(sequences, length_tokens, q_width)
    key_seq = key_b.reshape(sequences, length_tokens, kv_width)
    value_seq = value_b.reshape(sequences, length_tokens, kv_width)
    attended_rows, log_totals = lax.map(
        forward_one, (query_seq, key_seq, value_seq, document_index)
    )
    attended_all = attended_rows.reshape(group_rows, q_width)
    piece = attended_all
    middle = tokens_f + lax.psum_scatter(
        dot_right_t(piece, full_out).astype(jnp.bfloat16), "tensor", scatter_dimension=0, tiled=True
    ).astype(jnp.float32)
    inverse_two = lax.rsqrt(jnp.mean(middle * middle, axis=1, keepdims=True) + eps_norm)
    normed_two = (middle * inverse_two * gain_two_f).astype(jnp.bfloat16)
    normed_two_all = lax.all_gather(normed_two, "tensor", axis=0, tiled=True)
    expert_ids = jnp.arange(experts, dtype=jnp.int32)
    member = jnp.any(routes[:, :, None] == expert_ids[None, None, :], axis=1)
    logits_all = plain_dot(normed_two_all, router_full)
    masked_logits = jnp.where(member, logits_all, -jnp.inf)
    peak_logits = jnp.max(masked_logits, axis=1, keepdims=True)
    exp_logits = jnp.exp(masked_logits - peak_logits)
    gates_all_f = exp_logits / jnp.sum(exp_logits, axis=1, keepdims=True)
    hidden_expert = jnp.arange(experts * ff_local, dtype=jnp.int32) // ff_local
    spread = (expert_ids[:, None] == hidden_expert[None, :]).astype(jnp.bfloat16)
    gates_wide = plain_dot(gates_all_f.astype(jnp.bfloat16), spread).astype(jnp.bfloat16)
    gates_wide_f = gates_wide.astype(jnp.float32)
    gate_kept = plain_dot(normed_two_all, full_gate)
    up_kept = plain_dot(normed_two_all, full_up)
    sigma = jax.nn.sigmoid(gate_kept)
    swish = gate_kept * sigma
    active_f = swish * up_kept
    weighted = (active_f * gates_wide_f).astype(jnp.bfloat16)
    down_local = dot_left_t(moe_grads_all, weighted).astype(jnp.bfloat16)
    grad_down = lax.psum_scatter(down_local, "dp", scatter_dimension=0, tiled=True)
    moe_all = dot_right_t(weighted, full_down).astype(jnp.bfloat16)
    upstream = cotangent.astype(jnp.float32)
    folded = plain_dot(moe_grads_all, full_down)
    gates_grad_part = dot_right_t((active_f * folded).astype(jnp.bfloat16), spread)
    active_grad = folded * gates_wide_f
    gate_pre_grad = (active_grad * up_kept * sigma * (1.0 + gate_kept * (1.0 - sigma))).astype(
        jnp.bfloat16
    )
    up_pre_grad = (active_grad * swish).astype(jnp.bfloat16)
    gate_local = dot_left_t(normed_two_all, gate_pre_grad).astype(jnp.bfloat16)
    up_local = dot_left_t(normed_two_all, up_pre_grad).astype(jnp.bfloat16)
    rows_grad_all = dot_right_t(gate_pre_grad, full_gate) + dot_right_t(up_pre_grad, full_up)
    pad = jnp.zeros((group_rows, 128 - experts % 128), jnp.bfloat16)
    expert_sums = lax.psum_scatter(
        jnp.concatenate(
            [rows_grad_all.astype(jnp.bfloat16), moe_all, gates_grad_part.astype(jnp.bfloat16), pad],
            axis=1,
        ),
        "tensor",
        scatter_dimension=0,
        tiled=True,
    ).astype(jnp.float32)
    normed_two_grad = expert_sums[:, :width]
    output = (middle + expert_sums[:, width : 2 * width]).astype(jnp.bfloat16)
    gates_grad = expert_sums[:, 2 * width : 2 * width + experts]
    gates_f = lax.dynamic_slice_in_dim(gates_all_f, my_index * local_rows, local_rows, 0)
    inner = jnp.sum(gates_f * gates_grad, axis=1, keepdims=True)
    logits_grad = (gates_f * (gates_grad - inner)).astype(jnp.bfloat16)
    grad_gate = lax.psum_scatter(gate_local, "dp", scatter_dimension=0, tiled=True)
    grad_up = lax.psum_scatter(up_local, "dp", scatter_dimension=0, tiled=True)
    router_grad = dot_left_t(normed_two, logits_grad)
    normed_two_grad = normed_two_grad + dot_right_t(logits_grad, router_full)
    middle_part, gain_two_grad = norm_backward(middle, inverse_two, gain_two_f, normed_two_grad)
    middle_grad = upstream + middle_part
    piece = lax.all_gather(middle_grad.astype(jnp.bfloat16), "tensor", axis=0, tiled=True)
    mixed_grad = plain_dot(piece, full_out)
    out_weight_grad = dot_left_t(piece, attended_all)
    attended_grad_b = mixed_grad.astype(jnp.bfloat16).reshape(sequences, length_tokens, q_width)

    def backward_one(packed):
        query_s, key_s, value_s, segment_s, log_total, grad_s = packed
        masked = scores_of(query_s, key_s, segment_s)
        probs_f = jnp.exp(masked - log_total)
        probs = probs_f.astype(jnp.bfloat16)
        heads_of_query = query_s.reshape(length_tokens, heads_kv, query_group, HEAD_SIZE)
        heads_of_key = key_s.reshape(length_tokens, heads_kv, HEAD_SIZE)
        heads_of_value = value_s.reshape(length_tokens, heads_kv, HEAD_SIZE)
        grad_heads = grad_s.reshape(length_tokens, heads_kv, query_group, HEAD_SIZE)
        prob_grad = jnp.einsum(
            "qkgd,skd->kgqs", grad_heads, heads_of_value, preferred_element_type=jnp.float32
        )
        row_inner = jnp.sum(probs_f * prob_grad, axis=-1, keepdims=True)
        score_grad = (probs_f * (prob_grad - row_inner)).astype(jnp.bfloat16)
        query_grad = (
            jnp.einsum(
                "kgqs,skd->qkgd", score_grad, heads_of_key, preferred_element_type=jnp.float32
            )
            * scale
        )
        key_grad = (
            jnp.einsum(
                "kgqs,qkgd->skd", score_grad, heads_of_query, preferred_element_type=jnp.float32
            )
            * scale
        )
        value_grad = jnp.einsum(
            "kgqs,qkgd->skd", probs, grad_heads, preferred_element_type=jnp.float32
        )
        return (
            query_grad.reshape(length_tokens, q_width),
            key_grad.reshape(length_tokens, kv_width),
            value_grad.reshape(length_tokens, kv_width),
        )

    query_grad, key_grad, value_grad = lax.map(
        backward_one, (query_seq, key_seq, value_seq, document_index, log_totals, attended_grad_b)
    )
    query_pre_grad = rotate_pairs(
        query_grad.reshape(group_rows, q_width), token_positions, heads_q, -1.0
    ).astype(jnp.bfloat16)
    key_pre_grad = rotate_pairs(
        key_grad.reshape(group_rows, kv_width), token_positions, heads_kv, -1.0
    ).astype(jnp.bfloat16)
    value_pre_grad = value_grad.reshape(group_rows, kv_width).astype(jnp.bfloat16)
    joined_grad = jnp.concatenate([query_pre_grad, key_pre_grad, value_pre_grad], axis=1)
    joined_weight_grad = dot_left_t(normed_all, joined_grad)
    normed_one_part = dot_right_t(joined_grad, joined)
    gain_one_grad = jnp.sum(normed_one_part * (tokens_all_f * inverse_all), axis=0)
    normed_one_grad = lax.psum_scatter(
        normed_one_part.astype(jnp.bfloat16), "tensor", scatter_dimension=0, tiled=True
    ).astype(jnp.float32)
    tokens_part, _ = norm_backward(tokens_f, inverse_one, gain_one_f, normed_one_grad)
    grad_tokens = (middle_grad + tokens_part).astype(jnp.bfloat16)
    extra = jnp.concatenate([router_grad, gain_one_grad[:, None], gain_two_grad[:, None]], axis=1)
    extra = jnp.pad(extra, ((0, 0), (0, 128 - (experts + 2) % 128)))
    projections = lax.psum_scatter(
        jnp.concatenate([joined_weight_grad, out_weight_grad, extra], axis=1).astype(jnp.bfloat16),
        "dp",
        scatter_dimension=0,
        tiled=True,
    ).astype(jnp.float32)
    grad_query = projections[:, :q_width]
    grad_key = projections[:, q_width : q_width + kv_width]
    grad_value = projections[:, q_width + kv_width : joined_width]
    grad_out = projections[:, joined_width : joined_width + q_width]
    small = lax.psum_scatter(
        projections[:, joined_width + q_width :], "tensor", scatter_dimension=0, tiled=True
    )
    grad_router = small[:, :experts]
    grad_gain_attn = small[:, experts]
    grad_gain_moe = small[:, experts + 1]
    grad_gate, grad_up, grad_down = (
        piece.astype(jnp.float32).reshape(w_gate.shape) for piece in (grad_gate, grad_up, grad_down)
    )
    return (
        output,
        grad_tokens,
        grad_gain_attn,
        grad_gain_moe,
        grad_query,
        grad_key,
        grad_value,
        grad_out,
        grad_router,
        grad_gate,
        grad_up,
        grad_down,
    )


def solution(mesh):
    return jax.shard_map(
        body,
        mesh=mesh,
        in_specs=(
            P(("dp", "tensor"), None),
            P(("dp", "tensor"), None),
            P("dp", None),
            P("dp", None),
            P(("dp", "tensor")),
            P(("dp", "tensor")),
            P("dp", "tensor"),
            P("dp", "tensor"),
            P("dp", "tensor"),
            P("dp", "tensor"),
            P(("dp", "tensor"), None),
            P("dp", None, "tensor"),
            P("dp", None, "tensor"),
            P("dp", None, "tensor"),
        ),
        out_specs=(
            P(("dp", "tensor"), None),
            P(("dp", "tensor"), None),
            P(("dp", "tensor")),
            P(("dp", "tensor")),
            P("dp", "tensor"),
            P("dp", "tensor"),
            P("dp", "tensor"),
            P("dp", "tensor"),
            P(("dp", "tensor"), None),
            P("dp", None, "tensor"),
            P("dp", None, "tensor"),
            P("dp", None, "tensor"),
        ),
        check_vma=False,
    )
```

```python
import jax
import jax.numpy as jnp
from jax import lax
from jax.sharding import PartitionSpec as P

HEAD_SIZE = 64


eps_norm = 1e-06
rope_base = 10000.0


def plain_dot(left, right):
    return jnp.dot(left, right, preferred_element_type=jnp.float32)


def dot_right_t(left, right):
    return lax.dot_general(
        left, right, (((1,), (1,)), ((), ())), preferred_element_type=jnp.float32
    )


def dot_left_t(left, right):
    return lax.dot_general(
        left, right, (((0,), (0,)), ((), ())), preferred_element_type=jnp.float32
    )


def doc_positions(segment_row):
    places = jnp.arange(segment_row.shape[0], dtype=jnp.int32)
    before = jnp.sum((segment_row[None, :] < segment_row[:, None]).astype(jnp.int32), axis=1)
    return places - before


def rotate_pairs(field, token_positions, heads, sign):
    length_tokens = field.shape[0]
    half = HEAD_SIZE // 2
    freqs = rope_base ** (-2.0 * jnp.arange(half, dtype=jnp.float32) / HEAD_SIZE)
    angles = token_positions.astype(jnp.float32)[:, None] * freqs[None, :]
    cosine = jnp.cos(angles)[:, None, :]
    sine = sign * jnp.sin(angles)[:, None, :]
    shaped = field.reshape(length_tokens, heads, HEAD_SIZE)
    first = shaped[:, :, :half]
    second = shaped[:, :, half:]
    turned = jnp.concatenate(
        [first * cosine - second * sine, second * cosine + first * sine], axis=2
    )
    return turned.reshape(length_tokens, heads * HEAD_SIZE)


def norm_backward(field, inverse, gain, upstream):
    scaled = upstream * gain
    gain_grad = jnp.sum(upstream * field * inverse, axis=0)
    inner = jnp.mean(scaled * field, axis=1, keepdims=True)
    return (inverse * scaled - field * inverse**3 * inner, gain_grad)


def ring_of(size):
    if size % 2:
        return list(range(size))
    return list(range(0, size, 2)) + list(range(size - 1, 0, -2))


def ring_moves(ring, turn):
    size = len(ring)
    return [(ring[i], ring[(i + turn) % size]) for i in range(size)]


def ring_owner(ring, turn, back):
    size = len(ring)
    table = [0] * size
    for place in range(size):
        table[ring[place]] = ring[(place - turn * back) % size]
    return jnp.asarray(table, jnp.int32)[lax.axis_index("dp")]


class RingGather:
    def __init__(self, first, second, ring):
        self.ring, self.step, self.rows = ring, 0, first.shape[0]
        self.held = [first, second]
        self.full = [
            jnp.zeros((len(ring) * self.rows, piece.shape[1]), piece.dtype) for piece in self.held
        ]
        self.place()

    def place(self):
        for which, turn in ((0, 1), (1, -1)):
            owner = ring_owner(self.ring, turn, self.step)
            self.full[which] = lax.dynamic_update_slice_in_dim(
                self.full[which], self.held[which], owner * self.rows, 0
            )

    def advance(self, steps, field=None):
        for _ in range(min(steps, len(self.ring) - 1 - self.step)):
            self.step += 1
            self.held = [
                lax.ppermute(self.held[which], "dp", ring_moves(self.ring, turn))
                for which, turn in ((0, 1), (1, -1))
            ]
            self.place()
        if field is not None:
            field, self.held = lax.optimization_barrier((field, self.held))
        return field


class RingScatter:
    def __init__(self, first, second, ring):
        self.ring, self.step = ring, 0
        self.rows = first.shape[0] // len(ring)
        self.fields = (first, second)
        self.sums = [self.term(0, 1), self.term(1, -1)]

    def term(self, which, turn):
        owner = ring_owner(self.ring, turn, self.step + 1)
        return lax.dynamic_slice_in_dim(self.fields[which], owner * self.rows, self.rows, 0)

    def advance(self, steps, field=None):
        last = len(self.ring) - 1
        for _ in range(min(steps, last - self.step)):
            self.step += 1
            for which, turn in ((0, 1), (1, -1)):
                came = lax.ppermute(self.sums[which], "dp", ring_moves(self.ring, turn))
                total = came.astype(jnp.float32) + self.term(which, turn).astype(jnp.float32)
                self.sums[which] = total if self.step == last else total.astype(jnp.bfloat16)
        if field is not None:
            field, self.sums = lax.optimization_barrier((field, self.sums))
        return field


def body(
    tokens,
    cotangent,
    document_index,
    routes,
    gain_attn,
    gain_moe,
    w_query,
    key_weight,
    value_weight,
    w_out,
    w_router,
    w_gate,
    w_up,
    w_down,
):
    parts = lax.axis_size("tensor")
    local_rows = tokens.shape[0]
    group_rows = local_rows * parts
    width = tokens.shape[1]
    sequences = document_index.shape[0]
    length_tokens = document_index.shape[1]
    my_index = lax.axis_index("tensor")
    experts = w_gate.shape[1]
    scale = HEAD_SIZE ** (-0.5)
    ff_local = w_gate.shape[2]
    small_packed = jnp.concatenate([w_router, gain_attn[:, None], gain_moe[:, None]], axis=1)
    small_full = lax.all_gather(small_packed, ("dp", "tensor"), axis=0, tiled=True)
    router_full = small_full[:, :experts]
    gain_one_f = small_full[:, experts].astype(jnp.float32)
    gain_two_f = small_full[:, experts + 1].astype(jnp.float32)
    tokens_all = lax.all_gather(tokens, "tensor", axis=0, tiled=True)
    attn_full = lax.all_gather(
        jnp.concatenate([w_query, key_weight, value_weight, w_out], axis=1),
        "dp",
        axis=0,
        tiled=True,
    )
    q_width = w_query.shape[1]
    kv_width = key_weight.shape[1]
    joined_width = q_width + 2 * kv_width
    dp_size = lax.axis_size("dp")
    ring = ring_of(dp_size) if 2 < dp_size <= 16 else None
    flat_gate = w_gate.reshape(-1, experts * ff_local)
    flat_up = w_up.reshape(-1, experts * ff_local)
    flat_down = w_down.reshape(-1, experts * ff_local)
    full_gate = lax.all_gather(flat_gate, "dp", axis=0, tiled=True)
    if ring is None:
        full_up = lax.all_gather(flat_up, "dp", axis=0, tiled=True)
        full_down = lax.all_gather(flat_down, "dp", axis=0, tiled=True)
    else:
        gathering = RingGather(flat_up, flat_down, ring)
        attn_full = gathering.advance(2, attn_full)
    joined = attn_full[:, :joined_width]
    full_out = attn_full[:, joined_width:]
    moe_grads_all = lax.all_gather(cotangent, "tensor", axis=0, tiled=True)
    tokens_f = tokens.astype(jnp.float32)
    inverse_one = lax.rsqrt(jnp.mean(tokens_f * tokens_f, axis=1, keepdims=True) + eps_norm)
    tokens_all_f = tokens_all.astype(jnp.float32)
    inverse_all = lax.rsqrt(
        jnp.mean(tokens_all_f * tokens_all_f, axis=1, keepdims=True) + eps_norm
    )
    normed_all = (tokens_all_f * inverse_all * gain_one_f).astype(jnp.bfloat16)
    heads_q = q_width // HEAD_SIZE
    heads_kv = kv_width // HEAD_SIZE
    query_group = heads_q // heads_kv
    projected = plain_dot(normed_all, joined)
    token_positions = jax.vmap(doc_positions)(document_index).reshape(-1)
    query_b = rotate_pairs(projected[:, :q_width], token_positions, heads_q, 1.0).astype(
        jnp.bfloat16
    )
    key_b = rotate_pairs(
        projected[:, q_width : q_width + kv_width], token_positions, heads_kv, 1.0
    ).astype(jnp.bfloat16)
    value_b = projected[:, q_width + kv_width :].astype(jnp.bfloat16)

    def scores_of(query_s, key_s, segment_s):
        heads_of_query = query_s.reshape(length_tokens, heads_kv, query_group, HEAD_SIZE)
        heads_of_key = key_s.reshape(length_tokens, heads_kv, HEAD_SIZE)
        raw = (
            jnp.einsum(
                "qkgd,skd->kgqs", heads_of_query, heads_of_key, preferred_element_type=jnp.float32
            )
            * scale
        )
        places = jnp.arange(length_tokens, dtype=jnp.int32)
        allowed = (segment_s[None, :] == segment_s[:, None]) & (places[None, :] <= places[:, None])
        return jnp.where(allowed[None, None], raw, -1e30)

    def forward_one(packed):
        query_s, key_s, value_s, segment_s = packed
        masked = scores_of(query_s, key_s, segment_s)
        peak = jnp.max(masked, axis=-1, keepdims=True)
        weights = jnp.exp(masked - peak)
        total = jnp.sum(weights, axis=-1, keepdims=True)
        probs = (weights / total).astype(jnp.bfloat16)
        heads_of_value = value_s.reshape(length_tokens, heads_kv, HEAD_SIZE)
        mixed = jnp.einsum(
            "kgqs,skd->qkgd", probs, heads_of_value, preferred_element_type=jnp.float32
        )
        return (mixed.reshape(length_tokens, q_width).astype(jnp.bfloat16), peak + jnp.log(total))

    query_seq = query_b.reshape(sequences, length_tokens, q_width)
    key_seq = key_b.reshape(sequences, length_tokens, kv_width)
    value_seq = value_b.reshape(sequences, length_tokens, kv_width)
    attended_rows, log_totals = lax.map(
        forward_one, (query_seq, key_seq, value_seq, document_index)
    )
    attended_all = attended_rows.reshape(group_rows, q_width)
    piece = attended_all
    branch = dot_right_t(piece, full_out).astype(jnp.bfloat16)
    if ring is not None:
        branch = gathering.advance(3, branch)
        branch, full_gate = lax.optimization_barrier((branch, full_gate))
    branch = lax.psum_scatter(branch, "tensor", scatter_dimension=0, tiled=True)
    if ring is not None:
        branch = gathering.advance(1, branch)
    middle = tokens_f + branch.astype(jnp.float32)
    inverse_two = lax.rsqrt(jnp.mean(middle * middle, axis=1, keepdims=True) + eps_norm)
    normed_two = (middle * inverse_two * gain_two_f).astype(jnp.bfloat16)
    normed_two_all = lax.all_gather(normed_two, "tensor", axis=0, tiled=True)
    if ring is not None:
        gathering.advance(dp_size)
        full_up, full_down = gathering.full
    expert_ids = jnp.arange(experts, dtype=jnp.int32)
    member = jnp.any(routes[:, :, None] == expert_ids[None, None, :], axis=1)
    logits_all = plain_dot(normed_two_all, router_full)
    masked_logits = jnp.where(member, logits_all, -jnp.inf)
    peak_logits = jnp.max(masked_logits, axis=1, keepdims=True)
    exp_logits = jnp.exp(masked_logits - peak_logits)
    gates_all_f = exp_logits / jnp.sum(exp_logits, axis=1, keepdims=True)
    hidden_expert = jnp.arange(experts * ff_local, dtype=jnp.int32) // ff_local
    spread = (expert_ids[:, None] == hidden_expert[None, :]).astype(jnp.bfloat16)
    gates_wide = plain_dot(gates_all_f.astype(jnp.bfloat16), spread).astype(jnp.bfloat16)
    gates_wide_f = gates_wide.astype(jnp.float32)
    gate_kept = plain_dot(normed_two_all, full_gate)
    up_kept = plain_dot(normed_two_all, full_up)
    sigma = jax.nn.sigmoid(gate_kept)
    swish = gate_kept * sigma
    active_f = swish * up_kept
    weighted = (active_f * gates_wide_f).astype(jnp.bfloat16)
    down_local = dot_left_t(moe_grads_all, weighted).astype(jnp.bfloat16)
    grad_down = lax.psum_scatter(down_local, "dp", scatter_dimension=0, tiled=True)
    moe_all = dot_right_t(weighted, full_down).astype(jnp.bfloat16)
    upstream = cotangent.astype(jnp.float32)
    folded = plain_dot(moe_grads_all, full_down)
    gates_grad_part = dot_right_t((active_f * folded).astype(jnp.bfloat16), spread)
    active_grad = folded * gates_wide_f
    gate_pre_grad = (active_grad * up_kept * sigma * (1.0 + gate_kept * (1.0 - sigma))).astype(
        jnp.bfloat16
    )
    up_pre_grad = (active_grad * swish).astype(jnp.bfloat16)
    gate_local = dot_left_t(normed_two_all, gate_pre_grad).astype(jnp.bfloat16)
    up_local = dot_left_t(normed_two_all, up_pre_grad).astype(jnp.bfloat16)
    rows_grad_all = dot_right_t(gate_pre_grad, full_gate) + dot_right_t(up_pre_grad, full_up)
    pad = jnp.zeros((group_rows, 128 - experts % 128), jnp.bfloat16)
    to_sum = jnp.concatenate(
        [rows_grad_all.astype(jnp.bfloat16), moe_all, gates_grad_part.astype(jnp.bfloat16), pad],
        axis=1,
    )
    if ring is not None:
        scattering = RingScatter(gate_local, up_local, ring)
        to_sum = scattering.advance(1, to_sum)
        to_sum, grad_down = lax.optimization_barrier((to_sum, grad_down))
    expert_sums = lax.psum_scatter(to_sum, "tensor", scatter_dimension=0, tiled=True)
    if ring is not None:
        expert_sums = scattering.advance(3, expert_sums)
    expert_sums = expert_sums.astype(jnp.float32)
    normed_two_grad = expert_sums[:, :width]
    output = (middle + expert_sums[:, width : 2 * width]).astype(jnp.bfloat16)
    gates_grad = expert_sums[:, 2 * width : 2 * width + experts]
    gates_f = lax.dynamic_slice_in_dim(gates_all_f, my_index * local_rows, local_rows, 0)
    inner = jnp.sum(gates_f * gates_grad, axis=1, keepdims=True)
    logits_grad = (gates_f * (gates_grad - inner)).astype(jnp.bfloat16)
    if ring is None:
        grad_gate = lax.psum_scatter(gate_local, "dp", scatter_dimension=0, tiled=True)
        grad_up = lax.psum_scatter(up_local, "dp", scatter_dimension=0, tiled=True)
    else:
        scattering.advance(dp_size)
        grad_gate, grad_up = scattering.sums
    router_grad = dot_left_t(normed_two, logits_grad)
    normed_two_grad = normed_two_grad + dot_right_t(logits_grad, router_full)
    middle_part, gain_two_grad = norm_backward(middle, inverse_two, gain_two_f, normed_two_grad)
    middle_grad = upstream + middle_part
    piece = lax.all_gather(middle_grad.astype(jnp.bfloat16), "tensor", axis=0, tiled=True)
    mixed_grad = plain_dot(piece, full_out)
    out_weight_grad = dot_left_t(piece, attended_all)
    attended_grad_b = mixed_grad.astype(jnp.bfloat16).reshape(sequences, length_tokens, q_width)

    def backward_one(packed):
        query_s, key_s, value_s, segment_s, log_total, grad_s = packed
        masked = scores_of(query_s, key_s, segment_s)
        probs_f = jnp.exp(masked - log_total)
        probs = probs_f.astype(jnp.bfloat16)
        heads_of_query = query_s.reshape(length_tokens, heads_kv, query_group, HEAD_SIZE)
        heads_of_key = key_s.reshape(length_tokens, heads_kv, HEAD_SIZE)
        heads_of_value = value_s.reshape(length_tokens, heads_kv, HEAD_SIZE)
        grad_heads = grad_s.reshape(length_tokens, heads_kv, query_group, HEAD_SIZE)
        prob_grad = jnp.einsum(
            "qkgd,skd->kgqs", grad_heads, heads_of_value, preferred_element_type=jnp.float32
        )
        row_inner = jnp.sum(probs_f * prob_grad, axis=-1, keepdims=True)
        score_grad = (probs_f * (prob_grad - row_inner)).astype(jnp.bfloat16)
        query_grad = (
            jnp.einsum(
                "kgqs,skd->qkgd", score_grad, heads_of_key, preferred_element_type=jnp.float32
            )
            * scale
        )
        key_grad = (
            jnp.einsum(
                "kgqs,qkgd->skd", score_grad, heads_of_query, preferred_element_type=jnp.float32
            )
            * scale
        )
        value_grad = jnp.einsum(
            "kgqs,qkgd->skd", probs, grad_heads, preferred_element_type=jnp.float32
        )
        return (
            query_grad.reshape(length_tokens, q_width),
            key_grad.reshape(length_tokens, kv_width),
            value_grad.reshape(length_tokens, kv_width),
        )

    query_grad, key_grad, value_grad = lax.map(
        backward_one, (query_seq, key_seq, value_seq, document_index, log_totals, attended_grad_b)
    )
    query_pre_grad = rotate_pairs(
        query_grad.reshape(group_rows, q_width), token_positions, heads_q, -1.0
    ).astype(jnp.bfloat16)
    key_pre_grad = rotate_pairs(
        key_grad.reshape(group_rows, kv_width), token_positions, heads_kv, -1.0
    ).astype(jnp.bfloat16)
    value_pre_grad = value_grad.reshape(group_rows, kv_width).astype(jnp.bfloat16)
    joined_grad = jnp.concatenate([query_pre_grad, key_pre_grad, value_pre_grad], axis=1)
    joined_weight_grad = dot_left_t(normed_all, joined_grad)
    normed_one_part = dot_right_t(joined_grad, joined)
    gain_one_grad = jnp.sum(normed_one_part * (tokens_all_f * inverse_all), axis=0)
    normed_one_grad = lax.psum_scatter(
        normed_one_part.astype(jnp.bfloat16), "tensor", scatter_dimension=0, tiled=True
    ).astype(jnp.float32)
    tokens_part, _ = norm_backward(tokens_f, inverse_one, gain_one_f, normed_one_grad)
    grad_tokens = (middle_grad + tokens_part).astype(jnp.bfloat16)
    extra = jnp.concatenate([router_grad, gain_one_grad[:, None], gain_two_grad[:, None]], axis=1)
    extra = jnp.pad(extra, ((0, 0), (0, 128 - (experts + 2) % 128)))
    projections = lax.psum_scatter(
        jnp.concatenate([joined_weight_grad, out_weight_grad, extra], axis=1).astype(jnp.bfloat16),
        "dp",
        scatter_dimension=0,
        tiled=True,
    ).astype(jnp.float32)
    grad_query = projections[:, :q_width]
    grad_key = projections[:, q_width : q_width + kv_width]
    grad_value = projections[:, q_width + kv_width : joined_width]
    grad_out = projections[:, joined_width : joined_width + q_width]
    small = lax.psum_scatter(
        projections[:, joined_width + q_width :], "tensor", scatter_dimension=0, tiled=True
    )
    grad_router = small[:, :experts]
    grad_gain_attn = small[:, experts]
    grad_gain_moe = small[:, experts + 1]
    grad_gate, grad_up, grad_down = (
        piece.astype(jnp.float32).reshape(w_gate.shape) for piece in (grad_gate, grad_up, grad_down)
    )
    return (
        output,
        grad_tokens,
        grad_gain_attn,
        grad_gain_moe,
        grad_query,
        grad_key,
        grad_value,
        grad_out,
        grad_router,
        grad_gate,
        grad_up,
        grad_down,
    )


def solution(mesh):
    return jax.shard_map(
        body,
        mesh=mesh,
        in_specs=(
            P(("dp", "tensor"), None),
            P(("dp", "tensor"), None),
            P("dp", None),
            P("dp", None),
            P(("dp", "tensor")),
            P(("dp", "tensor")),
            P("dp", "tensor"),
            P("dp", "tensor"),
            P("dp", "tensor"),
            P("dp", "tensor"),
            P(("dp", "tensor"), None),
            P("dp", None, "tensor"),
            P("dp", None, "tensor"),
            P("dp", None, "tensor"),
        ),
        out_specs=(
            P(("dp", "tensor"), None),
            P(("dp", "tensor"), None),
            P(("dp", "tensor")),
            P(("dp", "tensor")),
            P("dp", "tensor"),
            P("dp", "tensor"),
            P("dp", "tensor"),
            P("dp", "tensor"),
            P(("dp", "tensor"), None),
            P("dp", None, "tensor"),
            P("dp", None, "tensor"),
            P("dp", None, "tensor"),
        ),
        check_vma=False,
    )
```
